512 devices in a mesh: row: 8 (over y, core), col: 16 (over z_hi, x), rep: 4 (over z_lo).
Axes of the slice: x: 4, y: 4, z: 16 (z_hi: 4, z_lo: 4; z = z_hi * 4 + z_lo), core: 2. Of those that a mesh axis runs over, the one named last changes fastest.
Arguments:
- amplitudes: bfloat16 [6144, 100, 1024], P(('row', 'col'), 'rep'), may hold values from -6 to 6
- integrals: bfloat16 [100, 1024, 1024], P('rep', 'col', 'row'), may hold values from -0.02734375 to 0.02734375
Outputs:
- cycle: float32 [6144, 1024], P('row', ('col', 'rep'))
The draws below stay inside these ranges and needn't reach their ends.
All inputs are finite; a program needn't handle non-finite values.
Results may differ from the reference program's by a relative error of at most 0.0003.
Values may be sent and summed in bfloat16 or wider, within the bound.
No kernel may reach another device: no remote copies, remote signals or barrier semaphores. Data moves between devices by JAX's collectives and lax.ppermute only.
A program may use at most 64 MiB of HBM per device.

```python
import jax
import jax.numpy as jnp
from jax import lax

O = 100
V = 1024
ROWS = 6144
COLS = 1024


def strengthened(array, key, source, target, blocks, factor):
    def block_of(position):
        return (jnp.arange(array.shape[position]) // (array.shape[position] // blocks)).reshape((-1,) + (1,) * (array.ndim - 1 - position))

    near = jax.random.permutation(key, blocks)[block_of(target)]
    other_side = (block_of(target) + blocks // 2) % blocks
    return jnp.where((block_of(source) == near) | (block_of(source) == other_side), factor * array, array)


def shard_levels(key, extent, shards, smallest, largest):
    level = 1.0
    for dim, parts in shards:
        steps = jax.random.uniform(jax.random.fold_in(jax.random.fold_in(key, 6), dim), (parts,), jnp.float32, smallest / len(shards), largest / len(shards))
        level = level * jnp.repeat(jnp.exp(steps), extent[dim] // parts).reshape((-1,) + (1,) * (len(extent) - 1 - dim))
    return level


def noise(own_key, dims, deviation, bound, split=(), kind=jnp.bfloat16):
    entries = deviation * jax.random.normal(own_key, dims, jnp.float32)
    if split:
        entries = entries * shard_levels(own_key, dims, split, -0.22, 0.18)
    return jnp.clip(entries, -bound, bound).astype(kind)


def gaussian_with(own_key, shape, spread, reach, cuts, heavy, held_as=jnp.bfloat16):
    entries = spread * jax.random.normal(own_key, shape, jnp.float32)
    if cuts:
        entries = entries * shard_levels(own_key, shape, cuts, -0.22, 0.18)
    return jnp.clip(strengthened(entries, jax.random.fold_in(own_key, 3), *heavy), -reach, reach).astype(held_as)


def setup_inputs(seed: int = 0) -> dict:
    arg_keys = jax.random.split(jax.random.key(seed), 3)
    amplitudes = noise(arg_keys[0], (ROWS, O, V), 1.0, 6.0, ((0, 128), (1, 4)))
    integrals = gaussian_with(arg_keys[1], (O, V, COLS), (O * V) ** -0.5, 0.02734375, ((0, 4), (1, 16), (2, 8)), (1, 2, 16, 2.0))
    return dict(amplitudes=amplitudes, integrals=integrals)


def reference(amplitudes, integrals):
    def accumulate(running, orbital):
        amp_slab = lax.dynamic_index_in_dim(amplitudes, orbital, 1, keepdims=False)
        int_slab = lax.dynamic_index_in_dim(integrals, orbital, 0, keepdims=False)
        running = running + jnp.dot(amp_slab, int_slab, preferred_element_type=jnp.float32)
        return running, None

    initial = jnp.zeros((ROWS, COLS), jnp.float32)
    result, unused = lax.scan(accumulate, initial, jnp.arange(O, dtype=jnp.int32))
    return result
```

```python
import jax
import jax.numpy as jnp
from jax import lax
from jax.experimental import pallas as pl
from jax.experimental.pallas import tpu as pltpu
from jax.sharding import Mesh, PartitionSpec as P

BF16 = jnp.bfloat16
F32 = jnp.float32
K = 25
PAIRS = 13
DEPTH = PAIRS * 128
ROWS = 48
VMEM = pl.BlockSpec(memory_space=pltpu.VMEM)
SMEM = pl.BlockSpec(memory_space=pltpu.SMEM)


def params():
    return pltpu.CompilerParams(vmem_limit_bytes=32 * 2**20)


def reorder_kernel(a_ref, src_ref, out_ref, perm_ref):
    perm_ref[...] = (lax.broadcasted_iota(jnp.int32, (1024, 1024), 0) == src_ref[...]).astype(BF16)
    for p in range(2):
        columns = []
        for parity in range(2):
            for zh in range(4):
                at = pl.ds(zh * 256 + p * 128, 128)
                planes = [
                    a_ref[k, :, at] if k < K else jnp.zeros((ROWS, 128), BF16)
                    for k in range(parity, 2 * PAIRS, 2)
                ]
                columns.append(jnp.concatenate(planes, axis=0))
        left = jnp.concatenate(columns, axis=1)
        for y in range(4):
            moved = jnp.dot(left, perm_ref[:, y * 256:(y + 1) * 256], preferred_element_type=F32).astype(BF16)
            for xb in range(2):
                out_ref[y * 4 + 2 * p + xb] = moved[:, xb * 128:(xb + 1) * 128]


def reorder(planes, src):
    return pl.pallas_call(
        reorder_kernel,
        out_shape=jax.ShapeDtypeStruct((16, PAIRS * ROWS, 128), BF16),
        in_specs=[VMEM, VMEM],
        out_specs=VMEM,
        scratch_shapes=[pltpu.VMEM((1024, 1024), BF16)],
        compiler_params=params(),
        cost_estimate=pl.CostEstimate(flops=2 * 624 * 2048 * 1024, bytes_accessed=5 * 2**20, transcendentals=0),
        name="reorder",
    )(planes, src)


def product_kernel(core_ref, a_ref, own_ref, other_ref, out_ref, right_ref):
    core = core_ref[0]
    mine = pl.ds(pl.multiple_of(core * 128, 128), 128)
    theirs = pl.ds(pl.multiple_of((1 - core) * 128, 128), 128)
    for k in range(K):
        for zh in range(4):
            rows = pl.ds(k * 64 + zh * 16, 16)
            right_ref[rows, mine] = own_ref[zh, k]
            right_ref[rows, theirs] = other_ref[zh, k]
    right_ref[pl.ds(K * 64, 64), :] = jnp.zeros((64, 256), BF16)
    for y in range(4):
        left = jnp.concatenate(
            [a_ref[4 * y:4 * y + 4, p * ROWS:(p + 1) * ROWS, :].reshape(192, 128) for p in range(PAIRS)], axis=1
        )
        block = jnp.dot(left, right_ref[...], preferred_element_type=F32)
        for x in range(4):
            part = block[:, x * 64:(x + 1) * 64]
            out_ref[y * 4 + x] = jnp.concatenate([part[:96], part[96:]], axis=1)


def product(core, a, own, other):
    return pl.pallas_call(
        product_kernel,
        out_shape=jax.ShapeDtypeStruct((16, 96, 128), F32),
        in_specs=[SMEM, VMEM, VMEM, VMEM],
        out_specs=VMEM,
        scratch_shapes=[pltpu.VMEM((DEPTH, 256), BF16)],
        compiler_params=params(),
        cost_estimate=pl.CostEstimate(flops=2 * 768 * DEPTH * 256, bytes_accessed=5 * 2**20, transcendentals=0),
        name="product",
    )(core, a, own, other)


def first_sum_kernel(*refs):
    out_ref = refs[-1]
    for zh in range(4):
        total = jnp.sum(refs[zh][...], axis=0)
        turned = total.T
        for zl in range(4):
            at = zl * 16
            out_ref[zh * 4 + zl, :16, :96] = turned[at:at + 16]
            out_ref[zh * 4 + zl, 16:, :96] = turned[64 + at:64 + at + 16]
            out_ref[zh * 4 + zl, :, 96:] = jnp.zeros((32, 32), F32)


def first_sum(parts):
    return pl.pallas_call(
        first_sum_kernel,
        out_shape=jax.ShapeDtypeStruct((16, 32, 128), F32),
        in_specs=[VMEM] * 4,
        out_specs=VMEM,
        compiler_params=params(),
        cost_estimate=pl.CostEstimate(flops=2**20, bytes_accessed=4 * 2**20, transcendentals=0),
        name="first_sum",
    )(*parts)


def last_sum_kernel(in_ref, out_ref):
    for zh in range(4):
        total = in_ref[4 * zh] + in_ref[4 * zh + 1] + in_ref[4 * zh + 2] + in_ref[4 * zh + 3]
        for half in range(2):
            out_ref[:, zh * 192 + half * 96:zh * 192 + half * 96 + 96] = total[half * 16:half * 16 + 16, :96]


def last_sum(parts):
    return pl.pallas_call(
        last_sum_kernel,
        out_shape=jax.ShapeDtypeStruct((16, 768), F32),
        in_specs=[VMEM],
        out_specs=VMEM,
        compiler_params=params(),
        cost_estimate=pl.CostEstimate(flops=2**16, bytes_accessed=2**19, transcendentals=0),
        name="last_sum",
    )(parts)


def source_of_lane():
    lane = jnp.arange(1024, dtype=jnp.int32)
    y, xb, parity, zh, i = lane // 256, lane // 128 % 2, lane // 64 % 2, lane // 16 % 4, lane % 16
    return (parity * 512 + zh * 128 + xb * 64 + y * 16 + i).reshape(1, 1024)


def local(amplitudes, integrals):
    core = lax.axis_index("core").astype(jnp.int32).reshape(1)
    by_y = integrals.reshape(K, 4, 16, 128).transpose(1, 0, 2, 3)
    blocks = lax.all_to_all(by_y, "y", 0, 0, tiled=True)
    gathered = lax.all_gather(blocks, "zh", axis=0, tiled=False)

    sent = reorder(amplitudes.transpose(1, 0, 2), source_of_lane())
    rows = lax.all_to_all(sent, ("y", "x"), 0, 0, tiled=True)

    swapped = lax.ppermute(gathered, "core", [(0, 1), (1, 0)])
    partial = [product(core, rows, gathered[:, c], swapped[:, c]) for c in range(4)]
    arrived = [lax.all_to_all(part, ("y", "x"), 0, 0, tiled=True) for part in partial]
    final = lax.all_to_all(first_sum(arrived), ("zh", "zl"), 0, 0, tiled=True)
    return last_sum(final).T


def solution(mesh):
    fine = Mesh(mesh.devices.reshape(4, 2, 4, 4, 4), ("y", "core", "zh", "x", "zl"))
    return jax.shard_map(
        local,
        mesh=fine,
        in_specs=(P(("y", "core", "zh", "x"), "zl", None), P("zl", ("zh", "x"), ("y", "core"))),
        out_specs=P(("y", "core"), ("zh", "x", "zl")),
        check_vma=False,
    )
```

```python
import jax
import jax.numpy as jnp
from jax import lax
from jax.experimental import pallas as pl
from jax.experimental.pallas import tpu as pltpu
from jax.sharding import Mesh, PartitionSpec as P

BF16 = jnp.bfloat16
F32 = jnp.float32
K = 25
PAIRS = 13
DEPTH = PAIRS * 128
ROWS = 48
VMEM = pl.BlockSpec(memory_space=pltpu.VMEM)
SMEM = pl.BlockSpec(memory_space=pltpu.SMEM)


def params():
    return pltpu.CompilerParams(vmem_limit_bytes=32 * 2**20)


def reorder_kernel(a_ref, src_ref, out_ref, perm_ref):
    perm_ref[...] = (lax.broadcasted_iota(jnp.int32, (1024, 1024), 0) == src_ref[...]).astype(BF16)
    for p in range(2):
        columns = []
        for parity in range(2):
            for zh in range(4):
                at = pl.ds(zh * 256 + p * 128, 128)
                planes = [
                    a_ref[k, :, at] if k < K else jnp.zeros((ROWS, 128), BF16)
                    for k in range(parity, 2 * PAIRS, 2)
                ]
                columns.append(jnp.concatenate(planes, axis=0))
        left = jnp.concatenate(columns, axis=1)
        for y in range(4):
            moved = jnp.dot(left, perm_ref[:, y * 256:(y + 1) * 256], preferred_element_type=F32).astype(BF16)
            for xb in range(2):
                out_ref[y * 4 + 2 * p + xb] = moved[:, xb * 128:(xb + 1) * 128]


def reorder(planes, src):
    return pl.pallas_call(
        reorder_kernel,
        out_shape=jax.ShapeDtypeStruct((16, PAIRS * ROWS, 128), BF16),
        in_specs=[VMEM, VMEM],
        out_specs=VMEM,
        scratch_shapes=[pltpu.VMEM((1024, 1024), BF16)],
        compiler_params=params(),
        cost_estimate=pl.CostEstimate(flops=2 * 624 * 2048 * 1024, bytes_accessed=5 * 2**20, transcendentals=0),
        name="reorder",
    )(planes, src)


def product_kernel(place_ref, a_ref, *refs):
    out_ref, right_ref = refs[-2:]
    core = place_ref[0]
    for near_ref, far_ref, whose in ((refs[0], refs[1], core), (refs[2], refs[3], 1 - core)):
        for j in range(4):
            lanes = pl.ds(pl.multiple_of(j * 256 + whose * 128, 128), 128)
            for k in range(K):
                for step, piece in ((0, near_ref[0, j, k]), (3, near_ref[1, j, k]),
                                    (1, near_ref[2, j, k]), (2, far_ref[j, k])):
                    right_ref[pl.ds(k * 64 + step * 16, 16), lanes] = piece
    right_ref[pl.ds(K * 64, 64), :] = jnp.zeros((64, 1024), BF16)
    for y in range(4):
        left = jnp.concatenate(
            [a_ref[4 * y:4 * y + 4, p * ROWS:(p + 1) * ROWS, :].reshape(192, 128) for p in range(PAIRS)], axis=1
        )
        block = jnp.dot(left, right_ref[...], preferred_element_type=F32)
        for x in range(4):
            for j in range(4):
                part = block[:, j * 256 + x * 64:j * 256 + (x + 1) * 64]
                out_ref[y * 4 + x, j * 96:(j + 1) * 96] = jnp.concatenate([part[:96], part[96:]], axis=1)


def product(place, a, near, far, near_other, far_other):
    return pl.pallas_call(
        product_kernel,
        out_shape=jax.ShapeDtypeStruct((16, 384, 128), F32),
        in_specs=[SMEM] + [VMEM] * 5,
        out_specs=VMEM,
        scratch_shapes=[pltpu.VMEM((DEPTH, 1024), BF16)],
        compiler_params=params(),
        cost_estimate=pl.CostEstimate(flops=2 * 768 * DEPTH * 1024, bytes_accessed=11 * 2**20, transcendentals=0),
        name="product",
    )(place, a, near, far, near_other, far_other)


def pack_kernel(in_ref, out_ref):
    for zh in range(4):
        turned = in_ref[zh * 96:(zh + 1) * 96].T
        for zl in range(4):
            at = zl * 16
            out_ref[zh * 4 + zl, :16, :96] = turned[at:at + 16]
            out_ref[zh * 4 + zl, 16:, :96] = turned[64 + at:64 + at + 16]
            out_ref[zh * 4 + zl, :, 96:] = jnp.zeros((32, 32), F32)


def pack(total):
    return pl.pallas_call(
        pack_kernel,
        out_shape=jax.ShapeDtypeStruct((16, 32, 128), F32),
        in_specs=[VMEM],
        out_specs=VMEM,
        compiler_params=params(),
        cost_estimate=pl.CostEstimate(flops=2**16, bytes_accessed=2**19, transcendentals=0),
        name="pack",
    )(total)


def last_sum_kernel(in_ref, out_ref):
    for zh in range(4):
        total = in_ref[4 * zh] + in_ref[4 * zh + 1] + in_ref[4 * zh + 2] + in_ref[4 * zh + 3]
        for half in range(2):
            out_ref[:, zh * 192 + half * 96:zh * 192 + half * 96 + 96] = total[half * 16:half * 16 + 16, :96]


def last_sum(parts):
    return pl.pallas_call(
        last_sum_kernel,
        out_shape=jax.ShapeDtypeStruct((16, 768), F32),
        in_specs=[VMEM],
        out_specs=VMEM,
        compiler_params=params(),
        cost_estimate=pl.CostEstimate(flops=2**16, bytes_accessed=2**19, transcendentals=0),
        name="last_sum",
    )(parts)


def source_of_lane(zh):
    lane = jnp.arange(1024, dtype=jnp.int32)
    y, xb, parity, step, i = lane // 256, lane // 128 % 2, lane // 64 % 2, lane // 16 % 4, lane % 16
    return (parity * 512 + (step + zh) % 4 * 128 + xb * 64 + y * 16 + i).reshape(1, 1024)


def shift(value, axis, by):
    return lax.ppermute(value, axis, [(i, (i + by) % 4) for i in range(4)])


def swap(value):
    return lax.ppermute(value, "core", [(0, 1), (1, 0)])


def local(amplitudes, integrals):
    core, zh = (lax.axis_index(a).astype(jnp.int32) for a in ("core", "zh"))
    place = core.reshape(1)
    by_y = integrals.reshape(K, 4, 16, 128).transpose(1, 0, 2, 3)
    own = lax.all_to_all(by_y, "y", 0, 0, tiled=True)
    sent = reorder(amplitudes.transpose(1, 0, 2), source_of_lane(zh))
    rows = lax.all_to_all(sent, ("y", "x"), 0, 0, tiled=True)

    below, above = shift(own, "zh", 1), shift(own, "zh", -1)
    near = jnp.stack([own, below, above])
    far = jnp.concatenate([shift(below[:, :13], "zh", 1), shift(above[:, 13:], "zh", -1)], axis=1)
    part = product(place, rows, near, far, swap(near), swap(far))
    arrived = lax.all_to_all(part, ("y", "x"), 0, 0, tiled=True)
    total = jnp.sum(arrived, axis=0)
    final = lax.all_to_all(pack(total), ("zh", "zl"), 0, 0, tiled=True)
    return last_sum(final).T


def solution(mesh):
    fine = Mesh(mesh.devices.reshape(4, 2, 4, 4, 4), ("y", "core", "zh", "x", "zl"))
    return jax.shard_map(
        local,
        mesh=fine,
        in_specs=(P(("y", "core", "zh", "x"), "zl", None), P("zl", ("zh", "x"), ("y", "core"))),
        out_specs=P(("y", "core"), ("zh", "x", "zl")),
        check_vma=False,
    )
```

```python
import jax
import jax.numpy as jnp
from jax import lax
from jax.experimental import pallas as pl
from jax.experimental.pallas import tpu as pltpu
from jax.sharding import Mesh, PartitionSpec as P

BF16 = jnp.bfloat16
F32 = jnp.float32
K = 25
PAIRS = 13
DEPTH = PAIRS * 128
ROWS = 48
VMEM = pl.BlockSpec(memory_space=pltpu.VMEM)
SMEM = pl.BlockSpec(memory_space=pltpu.SMEM)


def params():
    return pltpu.CompilerParams(vmem_limit_bytes=32 * 2**20)


def reorder_kernel(a_ref, src_ref, out_ref, perm_ref):
    perm_ref[...] = (lax.broadcasted_iota(jnp.int32, (1024, 1024), 0) == src_ref[...]).astype(BF16)
    for p in range(2):
        columns = []
        for parity in range(2):
            for zh in range(4):
                at = pl.ds(zh * 256 + p * 128, 128)
                planes = [
                    a_ref[k, :, at] if k < K else jnp.zeros((ROWS, 128), BF16)
                    for k in range(parity, 2 * PAIRS, 2)
                ]
                columns.append(jnp.concatenate(planes, axis=0))
        left = jnp.concatenate(columns, axis=1)
        for y in range(4):
            moved = jnp.dot(left, perm_ref[:, y * 256:(y + 1) * 256], preferred_element_type=F32).astype(BF16)
            for xb in range(2):
                out_ref[y * 4 + 2 * p + xb] = moved[:, xb * 128:(xb + 1) * 128]


def reorder(planes, src):
    return pl.pallas_call(
        reorder_kernel,
        out_shape=jax.ShapeDtypeStruct((16, PAIRS * ROWS, 128), BF16),
        in_specs=[VMEM, VMEM],
        out_specs=VMEM,
        scratch_shapes=[pltpu.VMEM((1024, 1024), BF16)],
        compiler_params=params(),
        cost_estimate=pl.CostEstimate(flops=2 * 624 * 2048 * 1024, bytes_accessed=5 * 2**20, transcendentals=0),
        name="reorder",
    )(planes, src)


def product_kernel(place_ref, a_ref, *refs):
    out_ref, right_ref = refs[-2:]
    core = place_ref[0]
    for near_ref, far_ref, whose in ((refs[0], refs[1], core), (refs[2], refs[3], 1 - core)):
        for j in range(4):
            lanes = pl.ds(pl.multiple_of(j * 256 + whose * 128, 128), 128)
            for k in range(K):
                for step, piece in ((0, near_ref[0, j, k]), (3, near_ref[1, j, k]),
                                    (1, near_ref[2, j, k]), (2, far_ref[j, k])):
                    right_ref[pl.ds(k * 64 + step * 16, 16), lanes] = piece
    right_ref[pl.ds(K * 64, 64), :] = jnp.zeros((64, 1024), BF16)
    for y in range(4):
        left = jnp.concatenate(
            [a_ref[4 * y:4 * y + 4, p * ROWS:(p + 1) * ROWS, :].reshape(192, 128) for p in range(PAIRS)], axis=1
        )
        block = jnp.dot(left, right_ref[...], preferred_element_type=F32)
        largest = jnp.max(jnp.max(jnp.abs(block), axis=0, keepdims=True), axis=1, keepdims=True)
        exponent = jnp.ceil(jnp.log2(jnp.maximum(largest, 2.0 ** -100)))
        block = block * jnp.exp2(7.0 - exponent)
        block = block * jnp.abs(block)
        for x in range(4):
            for j in range(4):
                part = block[:, j * 256 + x * 64:j * 256 + (x + 1) * 64]
                out_ref[y * 4 + x, j * 96:(j + 1) * 96] = jnp.concatenate([part[:96], part[96:]], axis=1)
            out_ref[y * 4 + x, 384:] = jnp.broadcast_to(exponent, (16, 128))


def product(place, a, near, far, near_other, far_other):
    return pl.pallas_call(
        product_kernel,
        out_shape=jax.ShapeDtypeStruct((16, 400, 128), F32),
        in_specs=[SMEM] + [VMEM] * 5,
        out_specs=VMEM,
        scratch_shapes=[pltpu.VMEM((DEPTH, 1024), BF16)],
        compiler_params=params(),
        cost_estimate=pl.CostEstimate(flops=2 * 768 * DEPTH * 1024, bytes_accessed=11 * 2**20, transcendentals=0),
        name="product",
    )(place, a, near, far, near_other, far_other)


def pack_kernel(in_ref, out_ref):
    for zh in range(4):
        turned = in_ref[zh * 96:(zh + 1) * 96].T
        for zl in range(4):
            at = zl * 16
            out_ref[zh * 4 + zl, :16, :96] = turned[at:at + 16]
            out_ref[zh * 4 + zl, 16:, :96] = turned[64 + at:64 + at + 16]
            out_ref[zh * 4 + zl, :, 96:] = jnp.zeros((32, 32), F32)


def pack(total):
    return pl.pallas_call(
        pack_kernel,
        out_shape=jax.ShapeDtypeStruct((16, 32, 128), F32),
        in_specs=[VMEM],
        out_specs=VMEM,
        compiler_params=params(),
        cost_estimate=pl.CostEstimate(flops=2**16, bytes_accessed=2**19, transcendentals=0),
        name="pack",
    )(total)


def last_sum_kernel(in_ref, out_ref):
    for zh in range(4):
        total = in_ref[4 * zh] + in_ref[4 * zh + 1] + in_ref[4 * zh + 2] + in_ref[4 * zh + 3]
        for half in range(2):
            out_ref[:, zh * 192 + half * 96:zh * 192 + half * 96 + 96] = total[half * 16:half * 16 + 16, :96]


def last_sum(parts):
    return pl.pallas_call(
        last_sum_kernel,
        out_shape=jax.ShapeDtypeStruct((16, 768), F32),
        in_specs=[VMEM],
        out_specs=VMEM,
        compiler_params=params(),
        cost_estimate=pl.CostEstimate(flops=2**16, bytes_accessed=2**19, transcendentals=0),
        name="last_sum",
    )(parts)


def source_of_lane(zh):
    lane = jnp.arange(1024, dtype=jnp.int32)
    y, xb, parity, step, i = lane // 256, lane // 128 % 2, lane // 64 % 2, lane // 16 % 4, lane % 16
    return (parity * 512 + (step + zh) % 4 * 128 + xb * 64 + y * 16 + i).reshape(1, 1024)


def shift(value, axis, by):
    return lax.ppermute(value, axis, [(i, (i + by) % 4) for i in range(4)])


def swap(value):
    return lax.ppermute(value, "core", [(0, 1), (1, 0)])


def local(amplitudes, integrals):
    core, zh = (lax.axis_index(a).astype(jnp.int32) for a in ("core", "zh"))
    place = core.reshape(1)
    by_y = integrals.reshape(K, 4, 16, 128).transpose(1, 0, 2, 3)
    own = lax.all_to_all(by_y, "y", 0, 0, tiled=True)
    sent = reorder(amplitudes.transpose(1, 0, 2), source_of_lane(zh))
    rows = lax.all_to_all(sent, ("y", "x"), 0, 0, tiled=True)

    below, above = shift(own, "zh", 1), shift(own, "zh", -1)
    near = jnp.stack([own, below, above])
    far = jnp.concatenate([shift(below[:, :13], "zh", 1), shift(above[:, 13:], "zh", -1)], axis=1)
    part = product(place, rows, near, far, swap(near), swap(far)).astype(jnp.float16)
    arrived = lax.all_to_all(part, ("y", "x"), 0, 0, tiled=True).astype(F32)
    scale = jnp.exp2(arrived[:, 384:385, :1] - 7.0)
    coded = arrived[:, :384]
    root = jnp.sqrt(jnp.abs(coded)) * scale
    total = jnp.sum(jnp.where(coded < 0, -root, root), axis=0)
    final = lax.all_to_all(pack(total), ("zh", "zl"), 0, 0, tiled=True)
    return last_sum(final).T


def solution(mesh):
    fine = Mesh(mesh.devices.reshape(4, 2, 4, 4, 4), ("y", "core", "zh", "x", "zl"))
    return jax.shard_map(
        local,
        mesh=fine,
        in_specs=(P(("y", "core", "zh", "x"), "zl", None), P("zl", ("zh", "x"), ("y", "core"))),
        out_specs=P(("y", "core"), ("zh", "x", "zl")),
        check_vma=False,
    )
```

```python
import jax
import jax.numpy as jnp
from jax import lax
from jax.experimental import pallas as pl
from jax.experimental.pallas import tpu as pltpu
from jax.sharding import Mesh, PartitionSpec as P

BF16 = jnp.bfloat16
F32 = jnp.float32
K = 25
PAIRS = 13
DEPTH = PAIRS * 128
ROWS = 48
VMEM = pl.BlockSpec(memory_space=pltpu.VMEM)
SMEM = pl.BlockSpec(memory_space=pltpu.SMEM)


def params():
    return pltpu.CompilerParams(vmem_limit_bytes=32 * 2**20)


def reorder_kernel(a_ref, src_ref, out_ref, perm_ref):
    perm_ref[...] = (lax.broadcasted_iota(jnp.int32, (1024, 1024), 0) == src_ref[...]).astype(BF16)
    for p in range(2):
        columns = []
        for parity in range(2):
            for zh in range(4):
                at = pl.ds(zh * 256 + p * 128, 128)
                planes = [
                    a_ref[k, :, at] if k < K else jnp.zeros((ROWS, 128), BF16)
                    for k in range(parity, 2 * PAIRS, 2)
                ]
                columns.append(jnp.concatenate(planes, axis=0))
        left = jnp.concatenate(columns, axis=1)
        for y in range(4):
            moved = jnp.dot(left, perm_ref[:, y * 256:(y + 1) * 256], preferred_element_type=F32).astype(BF16)
            for xb in range(2):
                out_ref[y * 4 + 2 * p + xb] = moved[:, xb * 128:(xb + 1) * 128]


def reorder(planes, src):
    return pl.pallas_call(
        reorder_kernel,
        out_shape=jax.ShapeDtypeStruct((16, PAIRS * ROWS, 128), BF16),
        in_specs=[VMEM, VMEM],
        out_specs=VMEM,
        scratch_shapes=[pltpu.VMEM((1024, 1024), BF16)],
        compiler_params=params(),
        cost_estimate=pl.CostEstimate(flops=2 * 624 * 2048 * 1024, bytes_accessed=5 * 2**20, transcendentals=0),
        name="reorder",
    )(planes, src)


def product_kernel(place_ref, a_ref, *refs):
    out_ref, right_ref = refs[-2:]
    core = place_ref[0]
    for near_ref, far_ref, whose in ((refs[0], refs[1], core), (refs[2], refs[3], 1 - core)):
        for j in range(4):
            lanes = pl.ds(pl.multiple_of(j * 256 + whose * 128, 128), 128)
            for k in range(K):
                for step, piece in ((0, near_ref[0, j, k]), (3, near_ref[1, j, k]),
                                    (1, near_ref[2, j, k]), (2, far_ref[j, k])):
                    right_ref[pl.ds(k * 64 + step * 16, 16), lanes] = piece
    right_ref[pl.ds(K * 64, 64), :] = jnp.zeros((64, 1024), BF16)
    for y in range(4):
        left = jnp.concatenate(
            [a_ref[4 * y:4 * y + 4, p * ROWS:(p + 1) * ROWS, :].reshape(192, 128) for p in range(PAIRS)], axis=1
        )
        block = jnp.dot(left, right_ref[...], preferred_element_type=F32)
        largest = jnp.max(jnp.max(jnp.abs(block), axis=0, keepdims=True), axis=1, keepdims=True)
        exponent = jnp.ceil(jnp.log2(jnp.maximum(largest, 2.0 ** -100)))
        block = block * jnp.exp2(7.0 - exponent)
        block = block * jnp.abs(block)
        for x in range(4):
            for j in range(4):
                part = block[:, j * 256 + x * 64:j * 256 + (x + 1) * 64]
                out_ref[y * 4 + x, j * 96:(j + 1) * 96] = jnp.concatenate([part[:96], part[96:]], axis=1)
            out_ref[y * 4 + x, 384:] = jnp.broadcast_to(exponent, (16, 128))


def product(place, a, near, far, near_other, far_other):
    return pl.pallas_call(
        product_kernel,
        out_shape=jax.ShapeDtypeStruct((16, 400, 128), F32),
        in_specs=[SMEM] + [VMEM] * 5,
        out_specs=VMEM,
        scratch_shapes=[pltpu.VMEM((DEPTH, 1024), BF16)],
        compiler_params=params(),
        cost_estimate=pl.CostEstimate(flops=2 * 768 * DEPTH * 1024, bytes_accessed=11 * 2**20, transcendentals=0),
        name="product",
    )(place, a, near, far, near_other, far_other)


def pack_kernel(in_ref, out_ref):
    for zh in range(4):
        turned = in_ref[zh * 96:(zh + 1) * 96].T
        for zl in range(4):
            low, high = turned[zl * 16:zl * 16 + 16], turned[64 + zl * 16:64 + zl * 16 + 16]
            out_ref[zh * 4 + zl, :16] = jnp.concatenate([low, high[:, :32]], axis=1)
            out_ref[zh * 4 + zl, 16:] = jnp.concatenate([high[:8, 32:], high[8:, 32:]], axis=1)


def pack(total):
    return pl.pallas_call(
        pack_kernel,
        out_shape=jax.ShapeDtypeStruct((16, 24, 128), F32),
        in_specs=[VMEM],
        out_specs=VMEM,
        compiler_params=params(),
        cost_estimate=pl.CostEstimate(flops=2**16, bytes_accessed=2**19, transcendentals=0),
        name="pack",
    )(total)


def last_sum_kernel(in_ref, out_ref):
    for zh in range(4):
        total = in_ref[4 * zh] + in_ref[4 * zh + 1] + in_ref[4 * zh + 2] + in_ref[4 * zh + 3]
        out_ref[:, zh * 192:zh * 192 + 128] = total[:16]
        out_ref[:8, zh * 192 + 128:zh * 192 + 192] = total[16:, :64]
        out_ref[8:, zh * 192 + 128:zh * 192 + 192] = total[16:, 64:]


def last_sum(parts):
    return pl.pallas_call(
        last_sum_kernel,
        out_shape=jax.ShapeDtypeStruct((16, 768), F32),
        in_specs=[VMEM],
        out_specs=VMEM,
        compiler_params=params(),
        cost_estimate=pl.CostEstimate(flops=2**16, bytes_accessed=2**19, transcendentals=0),
        name="last_sum",
    )(parts)


def source_of_lane(zh):
    lane = jnp.arange(1024, dtype=jnp.int32)
    y, xb, parity, step, i = lane // 256, lane // 128 % 2, lane // 64 % 2, lane // 16 % 4, lane % 16
    return (parity * 512 + (step + zh) % 4 * 128 + xb * 64 + y * 16 + i).reshape(1, 1024)


def shift(value, axis, by):
    return lax.ppermute(value, axis, [(i, (i + by) % 4) for i in range(4)])


def swap(value):
    return lax.ppermute(value, "core", [(0, 1), (1, 0)])


def local(amplitudes, integrals):
    core, zh = (lax.axis_index(a).astype(jnp.int32) for a in ("core", "zh"))
    place = core.reshape(1)
    by_y = integrals.reshape(K, 4, 16, 128).transpose(1, 0, 2, 3)
    own = lax.all_to_all(by_y, "y", 0, 0, tiled=True)
    sent = reorder(amplitudes.transpose(1, 0, 2), source_of_lane(zh))
    rows = lax.all_to_all(sent, ("y", "x"), 0, 0, tiled=True)

    first, second = own[:, :13], own[:, 13:]
    below, above = shift(first, "zh", 1), shift(second, "zh", -1)
    far = jnp.concatenate([shift(below, "zh", 1), shift(above, "zh", -1)], axis=1)
    below = jnp.concatenate([below, shift(second, "zh", 1)], axis=1)
    above = jnp.concatenate([shift(first, "zh", -1), above], axis=1)
    near, far = lax.optimization_barrier((jnp.stack([own, below, above]), far))
    part = product(place, rows, near, far, swap(near), swap(far)).astype(jnp.float16)
    arrived = lax.all_to_all(part, ("y", "x"), 0, 0, tiled=True).astype(F32)
    scale = jnp.exp2(arrived[:, 384:385, :1] - 7.0)
    coded = arrived[:, :384]
    root = jnp.sqrt(jnp.abs(coded)) * scale
    total = jnp.sum(jnp.where(coded < 0, -root, root), axis=0)
    final = lax.all_to_all(pack(total), ("zh", "zl"), 0, 0, tiled=True)
    return last_sum(final).T


def solution(mesh):
    fine = Mesh(mesh.devices.reshape(4, 2, 4, 4, 4), ("y", "core", "zh", "x", "zl"))
    return jax.shard_map(
        local,
        mesh=fine,
        in_specs=(P(("y", "core", "zh", "x"), "zl", None), P("zl", ("zh", "x"), ("y", "core"))),
        out_specs=P(("y", "core"), ("zh", "x", "zl")),
        check_vma=False,
    )
```

```python
import jax
import jax.numpy as jnp
from jax import lax
from jax.experimental import pallas as pl
from jax.experimental.pallas import tpu as pltpu
from jax.sharding import Mesh, PartitionSpec as P

BF16 = jnp.bfloat16
F32 = jnp.float32
K = 25
PAIRS = 13
DEPTH = PAIRS * 128
ROWS = 48
VMEM = pl.BlockSpec(memory_space=pltpu.VMEM)
SMEM = pl.BlockSpec(memory_space=pltpu.SMEM)


def params():
    return pltpu.CompilerParams(vmem_limit_bytes=32 * 2**20)


def reorder_kernel(a_ref, src_ref, out_ref, perm_ref):
    perm_ref[...] = (lax.broadcasted_iota(jnp.int32, (1024, 1024), 0) == src_ref[...]).astype(BF16)
    for p in range(2):
        columns = []
        for parity in range(2):
            for zh in range(4):
                at = pl.ds(zh * 256 + p * 128, 128)
                planes = [
                    a_ref[k, :, at] if k < K else jnp.zeros((ROWS, 128), BF16)
                    for k in range(parity, 2 * PAIRS, 2)
                ]
                columns.append(jnp.concatenate(planes, axis=0))
        left = jnp.concatenate(columns, axis=1)
        for y in range(4):
            moved = jnp.dot(left, perm_ref[:, y * 256:(y + 1) * 256], preferred_element_type=F32).astype(BF16)
            for xb in range(2):
                out_ref[y * 4 + 2 * p + xb] = moved[:, xb * 128:(xb + 1) * 128]


def reorder(planes, src):
    return pl.pallas_call(
        reorder_kernel,
        out_shape=jax.ShapeDtypeStruct((16, PAIRS * ROWS, 128), BF16),
        in_specs=[VMEM, VMEM],
        out_specs=VMEM,
        scratch_shapes=[pltpu.VMEM((1024, 1024), BF16)],
        compiler_params=params(),
        cost_estimate=pl.CostEstimate(flops=2 * 624 * 2048 * 1024, bytes_accessed=5 * 2**20, transcendentals=0),
        name="reorder",
    )(planes, src)


def product_kernel(place_ref, a_ref, *refs):
    out_ref, right_ref = refs[-2:]
    core = place_ref[0]
    for near_ref, far_ref, whose in ((refs[0], refs[1], core), (refs[2], refs[3], 1 - core)):
        for j in range(4):
            lanes = pl.ds(pl.multiple_of(j * 256 + whose * 128, 128), 128)
            for k in range(K):
                for step, piece in ((0, near_ref[0, j, k]), (3, near_ref[1, j, k]),
                                    (1, near_ref[2, j, k]), (2, far_ref[j, k])):
                    right_ref[pl.ds(k * 64 + step * 16, 16), lanes] = piece
    right_ref[pl.ds(K * 64, 64), :] = jnp.zeros((64, 1024), BF16)
    for y in range(4):
        left = jnp.concatenate(
            [a_ref[4 * y:4 * y + 4, p * ROWS:(p + 1) * ROWS, :].reshape(192, 128) for p in range(PAIRS)], axis=1
        )
        block = jnp.dot(left, right_ref[...], preferred_element_type=F32)
        for x in range(4):
            for j in range(4):
                part = block[:, j * 256 + x * 64:j * 256 + (x + 1) * 64]
                out_ref[y * 4 + x, j * 96:(j + 1) * 96] = jnp.concatenate([part[:96], part[96:]], axis=1)


def product(place, a, near, far, near_other, far_other):
    return pl.pallas_call(
        product_kernel,
        out_shape=jax.ShapeDtypeStruct((16, 384, 128), F32),
        in_specs=[SMEM] + [VMEM] * 5,
        out_specs=VMEM,
        scratch_shapes=[pltpu.VMEM((DEPTH, 1024), BF16)],
        compiler_params=params(),
        cost_estimate=pl.CostEstimate(flops=2 * 768 * DEPTH * 1024, bytes_accessed=11 * 2**20, transcendentals=0),
        name="product",
    )(place, a, near, far, near_other, far_other)


def pack_kernel(in_ref, out_ref):
    for zh in range(4):
        turned = in_ref[zh * 96:(zh + 1) * 96].T
        for zl in range(4):
            low, high = turned[zl * 16:zl * 16 + 16], turned[64 + zl * 16:64 + zl * 16 + 16]
            out_ref[zh * 4 + zl, :16] = jnp.concatenate([low, high[:, :32]], axis=1)
            out_ref[zh * 4 + zl, 16:] = jnp.concatenate([high[:8, 32:], high[8:, 32:]], axis=1)


def pack(total):
    return pl.pallas_call(
        pack_kernel,
        out_shape=jax.ShapeDtypeStruct((16, 24, 128), F32),
        in_specs=[VMEM],
        out_specs=VMEM,
        compiler_params=params(),
        cost_estimate=pl.CostEstimate(flops=2**16, bytes_accessed=2**19, transcendentals=0),
        name="pack",
    )(total)


def last_sum_kernel(in_ref, out_ref):
    for zh in range(4):
        total = in_ref[4 * zh] + in_ref[4 * zh + 1] + in_ref[4 * zh + 2] + in_ref[4 * zh + 3]
        out_ref[:, zh * 192:zh * 192 + 128] = total[:16]
        out_ref[:8, zh * 192 + 128:zh * 192 + 192] = total[16:, :64]
        out_ref[8:, zh * 192 + 128:zh * 192 + 192] = total[16:, 64:]


def last_sum(parts):
    return pl.pallas_call(
        last_sum_kernel,
        out_shape=jax.ShapeDtypeStruct((16, 768), F32),
        in_specs=[VMEM],
        out_specs=VMEM,
        compiler_params=params(),
        cost_estimate=pl.CostEstimate(flops=2**16, bytes_accessed=2**19, transcendentals=0),
        name="last_sum",
    )(parts)


def source_of_lane(zh):
    lane = jnp.arange(1024, dtype=jnp.int32)
    y, xb, parity, step, i = lane // 256, lane // 128 % 2, lane // 64 % 2, lane // 16 % 4, lane % 16
    return (parity * 512 + (step + zh) % 4 * 128 + xb * 64 + y * 16 + i).reshape(1, 1024)


def shift(value, axis, by):
    return lax.ppermute(value, axis, [(i, (i + by) % 4) for i in range(4)])


def swap(value):
    return lax.ppermute(value, "core", [(0, 1), (1, 0)])


def local(amplitudes, integrals):
    core, zh = (lax.axis_index(a).astype(jnp.int32) for a in ("core", "zh"))
    place = core.reshape(1)
    by_y = integrals.reshape(K, 4, 16, 128).transpose(1, 0, 2, 3)
    own = lax.all_to_all(by_y, "y", 0, 0, tiled=True)
    sent = reorder(amplitudes.transpose(1, 0, 2), source_of_lane(zh))
    rows = lax.all_to_all(sent, ("y", "x"), 0, 0, tiled=True)

    first, second = own[:, :13], own[:, 13:]
    below, above = shift(first, "zh", 1), shift(second, "zh", -1)
    far = jnp.concatenate([shift(below, "zh", 1), shift(above, "zh", -1)], axis=1)
    below = jnp.concatenate([below, shift(second, "zh", 1)], axis=1)
    above = jnp.concatenate([shift(first, "zh", -1), above], axis=1)
    near, far = lax.optimization_barrier((jnp.stack([own, below, above]), far))
    part = product(place, rows, near, far, swap(near), swap(far))
    arrived = lax.all_to_all(part, ("y", "x"), 0, 0, tiled=True)
    total = jnp.sum(arrived, axis=0)
    final = lax.all_to_all(pack(total), ("zh", "zl"), 0, 0, tiled=True)
    return last_sum(final).T


def solution(mesh):
    fine = Mesh(mesh.devices.reshape(4, 2, 4, 4, 4), ("y", "core", "zh", "x", "zl"))
    return jax.shard_map(
        local,
        mesh=fine,
        in_specs=(P(("y", "core", "zh", "x"), "zl", None), P("zl", ("zh", "x"), ("y", "core"))),
        out_specs=P(("y", "core"), ("zh", "x", "zl")),
        check_vma=False,
    )
```
